256 devices in a mesh: grp: 2 (over x_lo), tok: 8 (over x_hi, y), voc: 16 (over z, core).
Axes of the slice: x: 4 (x_hi: 2, x_lo: 2; x = x_hi * 2 + x_lo), y: 4, z: 8, core: 2. Of those that a mesh axis runs over, the one named last changes fastest.
Arguments:
- hidden: bfloat16 [2, 512, 4096], P('grp', 'tok'), may hold values from -110 to 110
- head: bfloat16 [2, 4096, 81920], P('grp', None, ('tok', 'voc')), may hold values from -0.09375 to 0.09375
- teacher: bfloat16 [512, 81920], P('grp', ('tok', 'voc')), may hold values from -250 to 250
- labels: int32 [512], P('grp'), may hold values from 0 to 81919
Outputs:
- hidden_grad: bfloat16 [2, 512, 4096], P('grp', ('tok', 'voc'))
- head_grad: bfloat16 [2, 4096, 81920], P('grp', None, ('tok', 'voc'))
The draws below stay inside these ranges and needn't reach their ends.
All inputs are finite; a program needn't handle non-finite values.
Results may differ from the reference program's by a relative error of at most 0.0034.
Values may be sent and summed in bfloat16 or wider, within the bound.
A program may use at most 128 MiB of HBM per device.

```python
import math
import jax
import jax.numpy as jnp
import numpy as np

D = 4096
TOKENS = 512
V = 81920


def draw_hidden(key, part):
    key = jax.random.fold_in(key, 11)
    key_values = jax.random.fold_in(key, 0)
    values = jnp.clip(jax.random.normal(key_values, (2, TOKENS, D), jnp.float32), -5.0, 5.0)
    return values.astype(jnp.bfloat16)


def draw_teacher(key, part):
    key = jax.random.fold_in(key, 23)
    key_values, key_rows, key_cols = jax.random.split(key, 3)
    column_scale = jnp.exp(jax.random.uniform(key_cols, (1, V), jnp.float32, jnp.log(0.6), jnp.log(6.0)))
    values = jnp.clip(jax.random.normal(key_values, (TOKENS, V), jnp.float32), -5.0, 5.0)
    row_scale = jnp.exp(jax.random.uniform(key_rows, (TOKENS, 1), jnp.float32, 0.0, jnp.log(8.0)))
    values = values * row_scale * column_scale
    return values.astype(jnp.bfloat16)


def set_ends(array, key, low, largest):
    index_at = [jax.random.randint(jax.random.fold_in(key, axis), (), 0, length) for axis, length in enumerate(array.shape)]
    main_axis = array.shape.index(max(array.shape))
    neighbour = index_at[:main_axis] + [(index_at[main_axis] + 1) % array.shape[main_axis]] + index_at[main_axis + 1:]
    return array.at[tuple(index_at)].set(low).at[tuple(neighbour)].set(largest)


def block_levels(own_key, dims, pieces, low, top_value):
    level = 1.0
    for axis_at, shards_of in pieces:
        steps = jax.random.uniform(jax.random.fold_in(jax.random.fold_in(own_key, 6), axis_at), (shards_of,), jnp.float32, low / len(pieces), top_value / len(pieces))
        level = level * jnp.repeat(jnp.exp(steps), dims[axis_at] // shards_of).reshape((-1,) + (1,) * (len(dims) - 1 - axis_at))
    return level


def wide_ids(rng, shape, count, lean):
    loads = [min(1 << octave, count + 1 - (1 << octave)) * (1 << 20) // math.isqrt((1 << octave) ** lean) + 1 for octave in range((count + 1).bit_length()) if 1 << octave <= count]
    scale = 1 + sum(loads) // (1 << 30)
    table = np.cumsum(np.array([max(1, weight // scale) for weight in loads]))
    lot = jax.random.randint(jax.random.fold_in(rng, 1), shape, 0, int(table[len(loads) - 1]))
    start = jnp.left_shift(1, jnp.searchsorted(jnp.asarray(table, jnp.int32), lot, side="right").astype(jnp.int32))
    rank = start - 1 + jax.random.randint(jax.random.fold_in(rng, 4), shape, 0, 1 << 30) % jnp.minimum(start, count + 1 - start)
    return jax.random.permutation(jax.random.fold_in(rng, 2), count)[rank].astype(jnp.int32)


def gaussian(own_key, extent, width, limit, cuts=(), kind=jnp.bfloat16):
    factor_of = block_levels(own_key, extent, cuts, -0.22, 0.18) if cuts else 1.0
    entries = jax.random.normal(own_key, extent, jnp.float32) * width * factor_of
    return jnp.minimum(jnp.maximum(entries, -limit), limit).astype(kind)


def setup_inputs(seed: int = 0) -> dict:
    arg_keys = jax.random.split(jax.random.key(seed), 5)
    hidden = draw_hidden(jax.random.fold_in(arg_keys[4], 71), 0)
    head = gaussian(arg_keys[1], (2, D, V), D ** -0.5, 0.09375, ((0, 2), (2, 128)))
    teacher = draw_teacher(jax.random.fold_in(arg_keys[4], 71), 0)
    labels = set_ends(wide_ids(arg_keys[3], (TOKENS,), V, 2), jax.random.fold_in(arg_keys[3], 3), 0, V - 1).astype(jnp.int32)
    return {"hidden": hidden, "head": head, "teacher": teacher, "labels": labels}


grad_scale = 32.0
kl_weight = 0.5


def row_softmax(values):
    top = jnp.max(values, axis=1, keepdims=True)
    expon = jnp.exp(values - top)
    return expon / jnp.sum(expon, axis=1, keepdims=True)


def reference(hidden, head, teacher, labels):
    teacher_prob = row_softmax(teacher.astype(jnp.float32))
    onehot = (jnp.arange(V, dtype=jnp.int32)[None, :] == labels[:, None]).astype(jnp.float32)
    hidden_out = []
    head_out = []
    for exit_index in range(2):
        logits = jnp.dot(hidden[exit_index], head[exit_index], preferred_element_type=jnp.float32)
        student_prob = row_softmax(logits)
        grad = (grad_scale * (student_prob - kl_weight * teacher_prob - (1.0 - kl_weight) * onehot)).astype(jnp.bfloat16)
        head_out.append(jnp.dot(hidden[exit_index].T, grad, preferred_element_type=jnp.float32).astype(jnp.bfloat16))
        hidden_out.append(jnp.dot(grad, head[exit_index].T, preferred_element_type=jnp.float32).astype(jnp.bfloat16))
    return jnp.stack(hidden_out), jnp.stack(head_out)
```

```python
import functools

import jax
import jax.numpy as jnp
from jax import lax
from jax.experimental import pallas as pl
from jax.experimental.pallas import tpu as pltpu
from jax.sharding import PartitionSpec as P

GRAD_SCALE = 32.0
KL_WEIGHT = 0.5
MESH = pl.DeviceIdType.MESH
F32 = jnp.float32
BF16 = jnp.bfloat16

NY = 4
NZ = 8
TOK = 2 * NY
VOC = 2 * NZ
ROWS = 64
HALF = NY * ROWS
TOKENS = 2 * HALF
COLS = 640
WIDE = 256
DHALF = 8 * WIDE


def spread(row):
    return jnp.broadcast_to(row, (128, 128)).T


def as_row(col):
    return jnp.broadcast_to(col, (128, 128)).T[0:1, :]


def merge(parts):
    tops = parts[:, 0:4, :]
    top = jnp.max(tops, axis=0)
    total = jnp.sum(parts[:, 4:8, :] * jnp.exp(tops - top[None]), axis=0)
    return jnp.concatenate([top, total], axis=0)


def kernel(
    hid_in, teach_in, lab_in, head_in, hg_out, ho_out,
    hid, head_v, head_sib, teach_sib, lab_sib, prob, base, grad_own, grad_sib,
    t_voc, t_tok, t_fin, s_voc, s_tok,
    part, ya_buf, qa_own, qa_send, xa_buf, xb_buf, qb, yb_buf, red, z_buf, fin_own, fin_sib, ho_buf,
    head_sem, ho_sem, g_s, g_r, ga_s, ga_r, gb_s, gb_r, d_s, d_r, misc_s, misc_r,
    tv_s, tv_r, tt_s, tt_r, sv_s, sv_r, st_s, st_r, gr_s, gr_r,
    ya_s, ya_r, xa_s, xa_r, xb_s, xb_r, yb_s, yb_r, z_s, z_r,
):
    g = lax.axis_index("grp")
    t = lax.axis_index("tok")
    v = lax.axis_index("voc")
    xh, y = t // NY, t % NY
    z, c = v // 2, v % 2
    sib = (g, t, z * 2 + (1 - c))
    xpart = (g, (1 - xh) * NY + y, v)
    gpart = (1 - g, t, v)

    def ydev(r):
        return (g, xh * NY + lax.rem(y + r, NY), v)

    def zdev(r):
        return (g, t, lax.rem(z + r, NZ) * 2 + c)

    def vdev(r):
        return (g, t, lax.rem(v + r, VOC))

    def tdev(r):
        return (g, lax.rem(t + r, TOK), v)

    def yfrom(r):
        return lax.rem(y + NY - r, NY)

    def rdma(src, dst, ss, rs, device):
        return pltpu.make_async_remote_copy(
            src_ref=src, dst_ref=dst, send_sem=ss, recv_sem=rs, device_id=device, device_id_type=MESH
        )

    def rows_of(col, yy):
        return pl.ds(pl.multiple_of((col * NY + yy) * ROWS, ROWS), ROWS)

    def head_copy(i):
        rows = pl.ds(i * 1024, 1024)
        return pltpu.make_async_copy(head_in.at[rows, :], head_v.at[rows, :], head_sem.at[i])

    for i in range(4):
        head_copy(i).start()

    barrier = pltpu.get_barrier_semaphore()
    for r in range(1, VOC):
        pl.semaphore_signal(barrier, inc=1, device_id=vdev(r), device_id_type=MESH)
    for r in range(1, TOK):
        pl.semaphore_signal(barrier, inc=1, device_id=tdev(r), device_id_type=MESH)
    pl.semaphore_signal(barrier, inc=1, device_id=gpart, device_id_type=MESH)

    own_rows = rows_of(xh, y)
    for k in range(16):
        hid[k, own_rows, :] = hid_in[:, k * WIDE : (k + 1) * WIDE]

    zero_row = jnp.zeros((1, 128), F32)
    tops, sums = [], []
    for b in range(2):
        vals = teach_in[b * 128 : (b + 1) * 128, :].astype(F32)
        top = jnp.max(vals, axis=1, keepdims=True)
        tops.append(as_row(top))
        sums.append(as_row(jnp.sum(jnp.exp(vals - top), axis=1, keepdims=True)))
    t_voc[0] = jnp.concatenate(tops + [zero_row, zero_row] + sums + [zero_row, zero_row], axis=0)

    pl.semaphore_wait(barrier, VOC + TOK - 1)

    own_chunks = pl.ds(pl.multiple_of(c * 8, 8), 8)
    a_chunks = pl.ds(pl.multiple_of(c * 8, 4), 4)
    b_chunks = pl.ds(pl.multiple_of(c * 8 + 4, 4), 4)

    def gather_first(r):
        here = hid.at[own_chunks, own_rows, :]
        return rdma(here, here, g_s.at[r], g_r.at[r], xpart if r == 0 else ydev(r))

    def gather_first_in(r):
        here = hid.at[own_chunks, rows_of(1 - xh, y) if r == 0 else rows_of(xh, yfrom(r)), :]
        return rdma(here, here, g_s.at[r], g_r.at[r], sib)

    def forward_a(r):
        here = hid.at[a_chunks, rows_of(1 - xh, y), :]
        return rdma(here, here, ga_s.at[r], ga_r.at[r], ydev(r))

    def forward_a_in(r):
        here = hid.at[a_chunks, rows_of(1 - xh, yfrom(r)), :]
        return rdma(here, here, ga_s.at[r], ga_r.at[r], sib)

    def forward_b(r):
        here = hid.at[b_chunks, rows_of(xh, yfrom(r)), :]
        return rdma(here, here, gb_s.at[r], gb_r.at[r], xpart)

    def forward_b_in(r):
        here = hid.at[b_chunks, rows_of(1 - xh, yfrom(r)), :]
        return rdma(here, here, gb_s.at[r], gb_r.at[r], sib)

    def to_sibling(i, core):
        if i == 0:
            part_at, rows = pl.ds(pl.multiple_of(core * 8, 8), 8), rows_of(1 - xh, y)
        elif i < 4:
            part_at, rows = pl.ds(pl.multiple_of(core * 8, 8), 8), rows_of(xh, yfrom(i))
        elif i < 7:
            part_at, rows = pl.ds(pl.multiple_of(core * 8, 4), 4), rows_of(1 - xh, yfrom(i - 3))
        else:
            part_at, rows = pl.ds(pl.multiple_of(core * 8 + 4, 4), 4), rows_of(1 - xh, yfrom(i - 6))
        here = hid.at[part_at, rows, :]
        return rdma(here, here, d_s.at[i], d_r.at[i], sib)

    def stat_voc(buf, ss, rs, r):
        return rdma(buf.at[0], buf.at[r], ss.at[r], rs.at[r], vdev(r))

    def stat_tok(buf, ss, rs, r):
        return rdma(buf.at[0], buf.at[r], ss.at[r], rs.at[r], tdev(r))

    for r in (0, 1, 3, 2):
        gather_first(r).start()
    for r in range(1, VOC):
        stat_voc(t_voc, tv_s, tv_r, r).start()

    sib_rows = pl.ds(pl.multiple_of((1 - c) * DHALF, DHALF), DHALF)
    head_swap = rdma(head_in.at[sib_rows, :], head_sib, misc_s.at[0], misc_r.at[0], sib)
    head_swap.start()
    lab_swap = rdma(lab_in, lab_sib, misc_s.at[1], misc_r.at[1], gpart)
    lab_swap.start()
    teach_swap = rdma(teach_in, teach_sib, misc_s.at[2], misc_r.at[2], gpart)

    gather_first_in(0).wait_recv()
    for r in (1, 3, 2):
        forward_a(r).start()
    to_sibling(0, c).start()
    for r in (1, 3, 2):
        gather_first_in(r).wait_recv()
        forward_b(r).start()
        to_sibling(r, c).start()
    teach_swap.start()

    for r in range(1, VOC):
        stat_voc(t_voc, tv_s, tv_r, r).wait_recv()
    t_tok[0] = merge(t_voc[...])
    for r in range(1, TOK):
        stat_tok(t_tok, tt_s, tt_r, r).start()

    for i in range(4):
        head_copy(i).wait()

    def logits_of(col):
        rows = pl.ds(pl.multiple_of(col * HALF, HALF), HALF)
        lhs = jnp.concatenate([hid[k, rows, :] for k in range(16)], axis=1)
        logits = jnp.dot(lhs, head_v[...], preferred_element_type=F32)
        top = jnp.max(logits, axis=1, keepdims=True)
        expo = jnp.exp(logits - top)
        prob[rows, :] = expo
        total = jnp.sum(expo, axis=1, keepdims=True)
        for b in range(2):
            at = slice(b * 128, (b + 1) * 128)
            s_voc[0, pl.ds(col * 2 + b, 1), :] = as_row(top[at])
            s_voc[0, pl.ds(4 + col * 2 + b, 1), :] = as_row(total[at])

    def logits_step(i, carry):
        @pl.when(i == 0)
        def _():
            for r in (1, 3, 2):
                to_sibling(r, 1 - c).wait_recv()

        @pl.when(i == 1)
        def _():
            to_sibling(0, 1 - c).wait_recv()
            for r in (1, 3, 2):
                forward_a_in(r).wait_recv()
                to_sibling(3 + r, c).start()
            for r in (1, 3, 2):
                forward_b_in(r).wait_recv()
                to_sibling(6 + r, c).start()
            for r in (1, 3, 2):
                to_sibling(3 + r, 1 - c).wait_recv()
                to_sibling(6 + r, 1 - c).wait_recv()

        logits_of(jnp.where(i == 0, xh, 1 - xh))
        return carry

    lax.fori_loop(0, 2, logits_step, 0)

    for r in range(1, VOC):
        stat_voc(s_voc, sv_s, sv_r, r).start()

    for r in range(1, TOK):
        stat_tok(t_tok, tt_s, tt_r, r).wait_recv()
    t_fin[0] = merge(t_tok[...])
    fin_swap = rdma(t_fin.at[0], t_fin.at[1], misc_s.at[3], misc_r.at[3], gpart)
    fin_swap.start()
    lab_swap.wait_recv()
    teach_swap.wait_recv()
    fin_swap.wait_recv()
    column_base = (t * VOC + v) * COLS
    for which in range(2):
        values = teach_in if which == 0 else teach_sib
        labels = lab_in if which == 0 else lab_sib
        row0 = (g if which == 0 else 1 - g) * 256
        for b in range(2):
            rows = pl.ds(pl.multiple_of(row0 + b * 128, 128), 128)
            top = spread(t_fin[which, b : b + 1, :])
            scale = KL_WEIGHT / spread(t_fin[which, 4 + b : 5 + b, :])
            label = spread(labels[b : b + 1, :])
            for n in range(COLS // 128):
                at = slice(n * 128, (n + 1) * 128)
                soft = jnp.exp(values[b * 128 : (b + 1) * 128, at].astype(F32) - top) * scale
                ids = column_base + n * 128 + lax.broadcasted_iota(jnp.int32, (128, 128), 1)
                base[rows, at] = soft + jnp.where(ids == label, 1.0 - KL_WEIGHT, 0.0)

    for r in range(1, VOC):
        stat_voc(s_voc, sv_s, sv_r, r).wait_recv()
    s_tok[0] = merge(s_voc[...])
    for r in range(1, TOK):
        stat_tok(s_tok, st_s, st_r, r).start()
    for r in range(1, TOK):
        stat_tok(s_tok, st_s, st_r, r).wait_recv()
    final = merge(s_tok[...])
    factor = jnp.exp(s_voc[0, 0:4, :] - final[0:4, :]) / final[4:8, :]

    def grad_swap(b):
        rows = pl.ds(b * 128, 128)
        return rdma(grad_own.at[rows, :], grad_sib.at[rows, :], gr_s.at[b], gr_r.at[b], sib)

    for b in range(4):
        rows = slice(b * 128, (b + 1) * 128)
        mat = spread(factor[b : b + 1, :])
        for n in range(COLS // 128):
            at = slice(n * 128, (n + 1) * 128)
            grad_own[rows, at] = (GRAD_SCALE * (prob[rows, at] * mat - base[rows, at])).astype(BF16)
        grad_swap(b).start()
    head_swap.wait_recv()
    for b in range(4):
        grad_swap(b).wait_recv()

    def product(j):
        lhs = jnp.concatenate([grad_own[...], grad_sib[...]], axis=1)
        own = head_v[pl.ds(pl.multiple_of(c * DHALF + j * WIDE, WIDE), WIDE), :]
        other = head_sib[pl.ds(pl.multiple_of(j * WIDE, WIDE), WIDE), :]
        rhs = jnp.concatenate([own, other], axis=1)
        out = lax.dot_general(lhs, rhs, (((1,), (1,)), ((), ())), preferred_element_type=F32)
        part[j] = out.astype(BF16).reshape(2, NY, ROWS, WIDE)

    def send_ya(i, r):
        return rdma(
            part.at[i, :, lax.rem(y + r, NY)], ya_buf.at[i, r - 1], ya_s.at[i, r], ya_r.at[i, r], ydev(r)
        )

    def send_xb(i):
        return rdma(part.at[4 + i, 1 - xh], xb_buf.at[i], xb_s.at[i], xb_r.at[i], xpart)

    def send_xa(i):
        return rdma(qa_send.at[i], xa_buf.at[i], xa_s.at[i], xa_r.at[i], xpart)

    def send_yb(i, r):
        return rdma(qb.at[i, lax.rem(y + r, NY)], yb_buf.at[i, r - 1], yb_s.at[i, r], yb_r.at[i, r], ydev(r))

    def send_z(i, r):
        rows = pl.ds(pl.multiple_of(lax.rem(z + r, NZ) * 8, 8), 8)
        return rdma(red.at[i, :, rows, :], z_buf.at[i, r - 1], z_s.at[i, r], z_r.at[i, r], zdev(r))

    def ho_copy(k):
        return pltpu.make_async_copy(
            ho_buf.at[k], ho_out.at[pl.ds(pl.multiple_of(k * WIDE, WIDE), WIDE), :], ho_sem.at[k]
        )

    def head_piece(k):
        out = lax.dot_general(
            hid[k], grad_own[...], (((0,), (0,)), ((), ())), preferred_element_type=F32
        )
        ho_buf[k] = out.astype(BF16)
        ho_copy(k).start()

    def step1(i, carry):
        product(i)
        for r in (1, 3, 2):
            send_ya(i, r).start()
        product(4 + i)
        send_xb(i).start()
        return carry

    lax.fori_loop(0, 4, step1, 0)

    def step2(i, carry):
        head_piece(2 * i)
        head_piece(2 * i + 1)
        for r in (1, 3, 2):
            send_ya(i, r).wait_recv()

        def column(col):
            total = part[i, col, y].astype(F32)
            for r in range(3):
                total = total + ya_buf[i, r, col].astype(F32)
            return total

        qa_own[i] = column(xh)
        qa_send[i] = column(1 - xh).astype(BF16)
        send_xa(i).start()
        send_xb(i).wait_recv()
        qb[i] = (part[4 + i, xh].astype(F32) + xb_buf[i].astype(F32)).astype(BF16)
        for r in (1, 3, 2):
            send_yb(i, r).start()
        return carry

    lax.fori_loop(0, 4, step2, 0)

    def step3(i, carry):
        head_piece(8 + 2 * i)
        head_piece(9 + 2 * i)
        send_xa(i).wait_recv()
        red[i, 0] = qa_own[i] + xa_buf[i].astype(F32)
        for r in (1, 3, 2):
            send_yb(i, r).wait_recv()
        total = qb[i, y].astype(F32)
        for r in range(3):
            total = total + yb_buf[i, r].astype(F32)
        red[i, 1] = total
        for r in (4, 3, 5, 2, 6, 1, 7):
            send_z(i, r).start()
        return carry

    lax.fori_loop(0, 4, step3, 0)

    def step4(i, carry):
        for r in range(1, NZ):
            send_z(i, r).wait_recv()
        rows = pl.ds(pl.multiple_of(z * 8, 8), 8)
        total = red[i, :, rows, :]
        for r in range(NZ - 1):
            total = total + z_buf[i, r]
        fin_own[:, i] = total
        return carry

    lax.fori_loop(0, 4, step4, 0)
    fin_core = rdma(fin_own, fin_sib, misc_s.at[4], misc_r.at[4], sib)
    fin_core.start()
    fin_core.wait_recv()
    first = c == 0
    for j in range(8):
        own = fin_own[j // 4, j % 4]
        other = fin_sib[j // 4, j % 4]
        own = jnp.where(first, own[0:4], own[4:8])
        other = jnp.where(first, other[0:4], other[4:8])
        low = jnp.where(first, own, other)
        high = jnp.where(first, other, own)
        hg_out[:, j * WIDE : (j + 1) * WIDE] = low.astype(BF16)
        hg_out[:, DHALF + j * WIDE : DHALF + (j + 1) * WIDE] = high.astype(BF16)

    for r in range(4):
        gather_first(r).wait_send()
    for r in range(1, 4):
        forward_a(r).wait_send()
        forward_b(r).wait_send()
    for i in range(10):
        to_sibling(i, c).wait_send()
    for r in range(1, VOC):
        stat_voc(t_voc, tv_s, tv_r, r).wait_send()
        stat_voc(s_voc, sv_s, sv_r, r).wait_send()
    for r in range(1, TOK):
        stat_tok(t_tok, tt_s, tt_r, r).wait_send()
        stat_tok(s_tok, st_s, st_r, r).wait_send()
    for copy in (head_swap, lab_swap, teach_swap, fin_swap, fin_core):
        copy.wait_send()
    for b in range(4):
        grad_swap(b).wait_send()

    def drain(i, carry):
        for r in range(1, 4):
            send_ya(i, r).wait_send()
            send_yb(i, r).wait_send()
        send_xa(i).wait_send()
        send_xb(i).wait_send()
        for r in range(1, NZ):
            send_z(i, r).wait_send()
        return carry

    lax.fori_loop(0, 4, drain, 0)

    def drain_head(k, carry):
        ho_copy(k).wait()
        return carry

    lax.fori_loop(0, 16, drain_head, 0)


def body(hidden, head, teacher, labels):
    dma = pltpu.SemaphoreType.DMA
    scratch = [
        pltpu.VMEM((16, TOKENS, WIDE), BF16),
        pltpu.VMEM((16 * WIDE, COLS), BF16),
        pltpu.VMEM((DHALF, COLS), BF16),
        pltpu.VMEM((256, COLS), BF16),
        pltpu.VMEM((2, 128), jnp.int32),
        pltpu.VMEM((TOKENS, COLS), F32),
        pltpu.VMEM((TOKENS, COLS), F32),
        pltpu.VMEM((TOKENS, COLS), BF16),
        pltpu.VMEM((TOKENS, COLS), BF16),
        pltpu.VMEM((VOC, 8, 128), F32),
        pltpu.VMEM((TOK, 8, 128), F32),
        pltpu.VMEM((2, 8, 128), F32),
        pltpu.VMEM((VOC, 8, 128), F32),
        pltpu.VMEM((TOK, 8, 128), F32),
        pltpu.VMEM((8, 2, NY, ROWS, WIDE), BF16),
        pltpu.VMEM((4, 3, 2, ROWS, WIDE), BF16),
        pltpu.VMEM((4, ROWS, WIDE), F32),
        pltpu.VMEM((4, ROWS, WIDE), BF16),
        pltpu.VMEM((4, ROWS, WIDE), BF16),
        pltpu.VMEM((4, NY, ROWS, WIDE), BF16),
        pltpu.VMEM((4, NY, ROWS, WIDE), BF16),
        pltpu.VMEM((4, 3, ROWS, WIDE), BF16),
        pltpu.VMEM((4, 2, ROWS, WIDE), F32),
        pltpu.VMEM((4, NZ - 1, 2, 8, WIDE), F32),
        pltpu.VMEM((2, 4, 8, WIDE), F32),
        pltpu.VMEM((2, 4, 8, WIDE), F32),
        pltpu.VMEM((16, WIDE, COLS), BF16),
        dma((4,)), dma((16,)),
        dma((4,)), dma((4,)), dma((4,)), dma((4,)), dma((4,)), dma((4,)),
        dma((10,)), dma((10,)), dma((5,)), dma((5,)),
        dma((VOC,)), dma((VOC,)), dma((TOK,)), dma((TOK,)),
        dma((VOC,)), dma((VOC,)), dma((TOK,)), dma((TOK,)),
        dma((4,)), dma((4,)),
        dma((4, 4)), dma((4, 4)), dma((4,)), dma((4,)),
        dma((4,)), dma((4,)), dma((4, 4)), dma((4, 4)),
        dma((4, NZ)), dma((4, NZ)),
    ]
    vmem = pl.BlockSpec(memory_space=pltpu.VMEM)
    hbm = pl.BlockSpec(memory_space=pl.ANY)
    hidden_out, head_out = pl.pallas_call(
        kernel,
        out_shape=(
            jax.ShapeDtypeStruct((4, 16 * WIDE), BF16),
            jax.ShapeDtypeStruct((16 * WIDE, COLS), BF16),
        ),
        in_specs=[vmem, vmem, vmem, hbm],
        out_specs=(vmem, hbm),
        scratch_shapes=scratch,
        compiler_params=pltpu.CompilerParams(
            collective_id=0, has_side_effects=True, vmem_limit_bytes=56 << 20
        ),
    )(hidden[0], teacher, labels.reshape(2, 128), head[0])
    return hidden_out[None], head_out[None]


def solution(mesh):
    placed = (
        P("grp", "tok", None),
        P("grp", None, ("tok", "voc")),
        P("grp", ("tok", "voc")),
        P("grp"),
    )
    return jax.shard_map(
        body,
        mesh=mesh,
        in_specs=placed,
        out_specs=(P("grp", ("tok", "voc"), None), P("grp", None, ("tok", "voc"))),
        check_vma=False,
    )
```

```python
import functools

import jax
import jax.numpy as jnp
from jax import lax
from jax.experimental import pallas as pl
from jax.experimental.pallas import tpu as pltpu
from jax.sharding import PartitionSpec as P

GRAD_SCALE = 32.0
KL_WEIGHT = 0.5
MESH = pl.DeviceIdType.MESH
F32 = jnp.float32
BF16 = jnp.bfloat16

NY = 4
NZ = 8
TOK = 2 * NY
VOC = 2 * NZ
ROWS = 64
HALF = NY * ROWS
TOKENS = 2 * HALF
COLS = 640
WIDE = 256
DHALF = 8 * WIDE


def spread(row):
    return jnp.broadcast_to(row, (128, 128)).T


def as_row(col):
    return jnp.broadcast_to(col, (128, 128)).T[0:1, :]


def merge(parts):
    tops = parts[:, 0:4, :]
    top = jnp.max(tops, axis=0)
    total = jnp.sum(parts[:, 4:8, :] * jnp.exp(tops - top[None]), axis=0)
    return jnp.concatenate([top, total], axis=0)


def kernel(
    hid_hbm, teach_hbm, lab_hbm, head_hbm, hg_out, ho_out,
    hid_in, teach_own, lab_own, hid, head_v, head_sib, teach_sib, lab_sib, prob, base, grad,
    t_voc, t_tok, t_fin, s_voc, s_tok,
    part, own, pair_buf, ya_buf, qa_own, qa_send, xa_buf, xb_buf, qb, qb_own, yb_buf, red, z_buf,
    fin_own, fin_sib, ho_buf,
    in_sem, ho_sem, h_s, h_r, misc_s, misc_r, tv_s, tv_r, tt_s, tt_r, sv_s, sv_r, st_s, st_r, pr_s, pr_r,
    pair_s, pair_r, ya_s, ya_r, xa_s, xa_r, xb_s, xb_r, yb_s, yb_r, z_s, z_r,
):
    g = lax.axis_index("grp")
    t = lax.axis_index("tok")
    v = lax.axis_index("voc")
    xh, y = t // NY, t % NY
    z, c = v // 2, v % 2
    parity = z % 2
    sib = (g, t, z * 2 + (1 - c))
    xpart = (g, (1 - xh) * NY + y, v)
    gpart = (1 - g, t, v)

    def ydev(r):
        return (g, xh * NY + lax.rem(y + r, NY), v)

    def zdev(r):
        return (g, t, lax.rem(z + r, NZ) * 2 + c)

    def vdev(r):
        return (g, t, lax.rem(v + r, VOC))

    def tdev(r):
        return (g, lax.rem(t + r, TOK), v)

    def yfrom(r):
        return lax.rem(y + NY - r, NY)

    def rdma(src, dst, ss, rs, device):
        return pltpu.make_async_remote_copy(
            src_ref=src, dst_ref=dst, send_sem=ss, recv_sem=rs, device_id=device, device_id_type=MESH
        )

    def rows_of(col, yy):
        return pl.ds(pl.multiple_of((col * NY + yy) * ROWS, ROWS), ROWS)

    barrier = pltpu.get_barrier_semaphore()
    for r in range(1, VOC):
        pl.semaphore_signal(barrier, inc=1, device_id=vdev(r), device_id_type=MESH)
    for r in range(1, TOK):
        pl.semaphore_signal(barrier, inc=1, device_id=tdev(r), device_id_type=MESH)
    pl.semaphore_signal(barrier, inc=1, device_id=gpart, device_id_type=MESH)

    loads = [
        pltpu.make_async_copy(hid_hbm, hid_in, in_sem.at[0]),
        pltpu.make_async_copy(teach_hbm, teach_own, in_sem.at[1]),
        pltpu.make_async_copy(lab_hbm, lab_own, in_sem.at[2]),
    ]
    for i in range(4):
        rows = pl.ds(i * 1024, 1024)
        loads.append(pltpu.make_async_copy(head_hbm.at[rows, :], head_v.at[rows, :], in_sem.at[3 + i]))
    for load in loads:
        load.start()

    own_rows = rows_of(xh, y)
    loads[0].wait()
    for k in range(16):
        hid[k, own_rows, :] = hid_in[:, k * WIDE : (k + 1) * WIDE]
    loads[1].wait()
    loads[2].wait()

    zero_row = jnp.zeros((1, 128), F32)
    tops, sums = [], []
    for b in range(2):
        vals = teach_own[b * 128 : (b + 1) * 128, :].astype(F32)
        top = jnp.max(vals, axis=1, keepdims=True)
        tops.append(as_row(top))
        sums.append(as_row(jnp.sum(jnp.exp(vals - top), axis=1, keepdims=True)))
    t_voc[0] = jnp.concatenate(tops + [zero_row, zero_row] + sums + [zero_row, zero_row], axis=0)

    pl.semaphore_wait(barrier, VOC + TOK - 1)

    sends = []

    def go(here, device):
        i = len(sends)
        copy = rdma(here, here, h_s.at[i], h_r.at[i], device)
        copy.start()
        sends.append(copy)
        return copy

    first = c * 8 + parity * 4
    other = c * 8 + (1 - parity) * 4

    def chunks(start, n):
        return pl.ds(pl.multiple_of(start, 2), n)

    x_in = go(hid.at[chunks(first, 4), own_rows, :], xpart)
    y_in = {r: go(hid.at[chunks(first, 4), own_rows, :], ydev(r)) for r in (1, 3, 2)}

    def stat_voc(buf, ss, rs, r):
        return rdma(buf.at[0], buf.at[r], ss.at[r], rs.at[r], vdev(r))

    def stat_tok(buf, ss, rs, r):
        return rdma(buf.at[0], buf.at[r], ss.at[r], rs.at[r], tdev(r))

    for r in range(1, VOC):
        stat_voc(t_voc, tv_s, tv_r, r).start()
    sib_rows = pl.ds(pl.multiple_of((1 - c) * DHALF, DHALF), DHALF)
    head_swap = rdma(head_hbm.at[sib_rows, :], head_sib, misc_s.at[0], misc_r.at[0], sib)
    head_swap.start()
    lab_swap = rdma(lab_own, lab_sib, misc_s.at[1], misc_r.at[1], gpart)
    lab_swap.start()
    teach_swap = rdma(teach_own, teach_sib, misc_s.at[2], misc_r.at[2], gpart)

    near, far, z_in = [], [], []

    def share(start, n, rows, arrivals):
        arrivals.append(go(hid.at[chunks(start, n), rows, :], sib))

    def along_z(rows, arrivals, up, down):
        if up:
            copy = go(hid.at[chunks(first, 2), rows, :], zdev(1))
            z_in.append((copy, other, rows, arrivals))
        if down:
            copy = go(hid.at[chunks(first + 2, 2), rows, :], zdev(NZ - 1))
            z_in.append((copy, other + 2, rows, arrivals))

    x_in.wait_recv()
    mirror = rows_of(1 - xh, y)
    a_in = {r: go(hid.at[chunks(first, 2), mirror, :], ydev(r)) for r in (1, 3, 2)}
    along_z(mirror, far, True, True)
    share(first, 4, mirror, far)
    b_in = {}
    for r in (1, 3, 2):
        y_in[r].wait_recv()
        rows = rows_of(xh, yfrom(r))
        b_in[r] = go(hid.at[chunks(first + 2, 2), rows, :], xpart)
        along_z(rows, near, True, True)
        share(first, 4, rows, near)
    teach_swap.start()
    for r in range(1, VOC):
        stat_voc(t_voc, tv_s, tv_r, r).wait_recv()
    t_tok[0] = merge(t_voc[...])
    for r in range(1, TOK):
        stat_tok(t_tok, tt_s, tt_r, r).start()
    for r in (1, 3, 2):
        rows = rows_of(1 - xh, yfrom(r))
        a_in[r].wait_recv()
        along_z(rows, far, True, False)
        share(first, 2, rows, far)
        b_in[r].wait_recv()
        along_z(rows, far, False, True)
        share(first + 2, 2, rows, far)
    for r in range(1, TOK):
        stat_tok(t_tok, tt_s, tt_r, r).wait_recv()
    t_fin[0] = merge(t_tok[...])
    fin_swap = rdma(t_fin.at[0], t_fin.at[1], misc_s.at[3], misc_r.at[3], gpart)
    fin_swap.start()
    for copy, start, rows, arrivals in z_in:
        copy.wait_recv()
        share(start, 2, rows, arrivals)
    for load in loads[3:]:
        load.wait()

    def prob_swap(i, col):
        here = prob.at[c, pl.ds(pl.multiple_of(col * HALF, HALF), HALF), :]
        return rdma(here, here, pr_s.at[i], pr_r.at[i], sib)

    def logits_step(i, carry):
        @pl.when(i == 0)
        def _():
            for copy in near:
                copy.wait_recv()

        @pl.when(i == 1)
        def _():
            for copy in far:
                copy.wait_recv()

        col = jnp.where(i == 0, xh, 1 - xh)
        rows = pl.ds(pl.multiple_of(col * HALF, HALF), HALF)
        lhs = jnp.concatenate([hid[k, rows, :] for k in range(16)], axis=1)
        logits = jnp.dot(lhs, head_v[...], preferred_element_type=F32)
        top = jnp.max(logits, axis=1, keepdims=True)
        expo = jnp.exp(logits - top)
        prob[c, rows, :] = expo
        prob_swap(i, col).start()
        total = jnp.sum(expo, axis=1, keepdims=True)
        for b in range(2):
            at = slice(b * 128, (b + 1) * 128)
            s_voc[0, pl.ds(col * 2 + b, 1), :] = as_row(top[at])
            s_voc[0, pl.ds(4 + col * 2 + b, 1), :] = as_row(total[at])
        return carry

    lax.fori_loop(0, 2, logits_step, 0)

    for r in range(1, VOC):
        stat_voc(s_voc, sv_s, sv_r, r).start()

    lab_swap.wait_recv()
    teach_swap.wait_recv()
    fin_swap.wait_recv()
    column_base = (t * VOC + v) * COLS
    base_swaps = []
    for which in range(2):
        values = teach_own if which == 0 else teach_sib
        labels = lab_own if which == 0 else lab_sib
        row0 = (g if which == 0 else 1 - g) * 256
        for b in range(2):
            rows = pl.ds(pl.multiple_of(row0 + b * 128, 128), 128)
            top = spread(t_fin[which, b : b + 1, :])
            scale = KL_WEIGHT / spread(t_fin[which, 4 + b : 5 + b, :])
            label = spread(labels[b : b + 1, :])
            for n in range(COLS // 128):
                at = slice(n * 128, (n + 1) * 128)
                soft = jnp.exp(values[b * 128 : (b + 1) * 128, at].astype(F32) - top) * scale
                ids = column_base + n * 128 + lax.broadcasted_iota(jnp.int32, (128, 128), 1)
                base[c, rows, at] = soft + jnp.where(ids == label, 1.0 - KL_WEIGHT, 0.0)
        here = base.at[c, pl.ds(pl.multiple_of(row0, 256), 256), :]
        base_swaps.append(rdma(here, here, pr_s.at[2 + which], pr_r.at[2 + which], sib))
        base_swaps[-1].start()

    for r in range(1, VOC):
        stat_voc(s_voc, sv_s, sv_r, r).wait_recv()
    s_tok[0] = merge(s_voc[...])
    for r in range(1, TOK):
        stat_tok(s_tok, st_s, st_r, r).start()
    head_swap.wait_recv()
    prob_swap(0, xh).wait_recv()
    prob_swap(1, 1 - xh).wait_recv()
    for copy in base_swaps:
        copy.wait_recv()
    for r in range(1, TOK):
        stat_tok(s_tok, st_s, st_r, r).wait_recv()
    final = merge(s_tok[...])
    sib_slot = jnp.where(c == 1, 1, VOC - 1)
    for which in range(2):
        tops = s_voc[0, 0:4, :] if which == 0 else s_voc[sib_slot, 0:4, :]
        core = c if which == 0 else 1 - c
        factor = jnp.exp(tops - final[0:4, :]) / final[4:8, :]
        for b in range(4):
            rows = slice(b * 128, (b + 1) * 128)
            mat = spread(factor[b : b + 1, :])
            for n in range(COLS // 128):
                at = slice(n * 128, (n + 1) * 128)
                out = GRAD_SCALE * (prob[core, rows, at] * mat - base[core, rows, at])
                grad[rows, which * COLS + n * 128 : which * COLS + (n + 1) * 128] = out.astype(BF16)

    def chunk_of(i):
        return jnp.where(i < 2, (1 - parity) * 2 + i, jnp.where(i < 6, i + 2, parity * 2 + i - 6))

    def send_pair(i):
        return rdma(part.at[i], pair_buf.at[i], pair_s.at[i], pair_r.at[i], zdev(1 if i == 0 else NZ - 1))

    def send_ya(k, r):
        return rdma(
            part.at[2 + 2 * k, :, lax.rem(y + r, NY)], ya_buf.at[k, r - 1], ya_s.at[k, r], ya_r.at[k, r], ydev(r)
        )

    def send_xb(k):
        return rdma(part.at[3 + 2 * k, 1 - xh], xb_buf.at[k], xb_s.at[k], xb_r.at[k], xpart)

    def send_xa(k):
        return rdma(qa_send.at[k], xa_buf.at[k], xa_s.at[k], xa_r.at[k], xpart)

    def send_yb(k, r):
        return rdma(qb.at[k, lax.rem(y + r, NY)], yb_buf.at[k, r - 1], yb_s.at[k, r], yb_r.at[k, r], ydev(r))

    def send_z(k, r):
        rows = pl.ds(pl.multiple_of(lax.rem(z + r, NZ) * 8, 8), 8)
        return rdma(red.at[k, :, rows, :], z_buf.at[k, r - 1], z_s.at[k, r], z_r.at[k, r], zdev(r))

    def ho_copy(k):
        return pltpu.make_async_copy(
            ho_buf.at[k], ho_out.at[pl.ds(pl.multiple_of(k * WIDE, WIDE), WIDE), :], ho_sem.at[k]
        )

    def head_pieces(start, n):
        def piece(k, carry):
            out = lax.dot_general(
                hid[k], grad[:, 0:COLS], (((0,), (0,)), ((), ())), preferred_element_type=F32
            )
            ho_buf[k] = out.astype(BF16)
            ho_copy(k).start()
            return carry

        lax.fori_loop(start, start + n, piece, 0)

    def product(i, carry):
        j = chunk_of(i)
        left = head_v[pl.ds(pl.multiple_of(c * DHALF + j * WIDE, WIDE), WIDE), :]
        right = head_sib[pl.ds(pl.multiple_of(j * WIDE, WIDE), WIDE), :]
        rhs = jnp.concatenate([left, right], axis=1)
        out = lax.dot_general(grad[...], rhs, (((1,), (1,)), ((), ())), preferred_element_type=F32)
        out = out.reshape(2, NY, ROWS, WIDE)
        own[i] = out
        part[i] = out.astype(BF16)

        for n in range(2):

            @pl.when(i == n)
            def _():
                send_pair(n).start()

            @pl.when(i == 2 + 2 * n)
            def _():
                for r in (1, 3, 2):
                    send_ya(n, r).start()

            @pl.when(i == 3 + 2 * n)
            def _():
                send_xb(n).start()

        return carry

    lax.fori_loop(0, 8, product, 0)

    def second(k, carry):
        for r in (1, 3, 2):
            send_ya(k, r).wait_recv()

        def column(col):
            total = own[2 + 2 * k, col, y]
            for r in range(3):
                total = total + ya_buf[k, r, col].astype(F32)
            return total

        qa_send[k] = column(1 - xh).astype(BF16)
        send_xa(k).start()
        qa_own[k] = column(xh)
        send_xb(k).wait_recv()
        qb[k] = (own[3 + 2 * k, xh] + xb_buf[k].astype(F32)).astype(BF16)
        for r in (1, 3, 2):
            send_yb(k, r).start()
        qb_own[k] = own[3 + 2 * k, xh, y] + xb_buf[k, y].astype(F32)
        return carry

    def third(k, carry):
        send_xa(k).wait_recv()
        red[k, 0] = qa_own[k] + xa_buf[k].astype(F32)
        for r in (1, 3, 2):
            send_yb(k, r).wait_recv()
        total = qb_own[k]
        for r in range(3):
            total = total + yb_buf[k, r].astype(F32)
        red[k, 1] = total
        for r in (4, 3, 5, 2, 6, 1, 7):
            send_z(k, r).start()
        return carry

    head_pieces(0, 4)
    lax.fori_loop(0, 2, second, 0)
    for n in range(2):
        send_pair(n).wait_recv()
        total = own[6 + n] + pair_buf[n].astype(F32)
        own[6 + n] = total
        part[6 + n] = total.astype(BF16)
        if n == 0:
            for r in (1, 3, 2):
                send_ya(2, r).start()
        else:
            send_xb(2).start()
    head_pieces(4, 4)
    lax.fori_loop(0, 2, third, 0)
    head_pieces(8, 4)
    lax.fori_loop(2, 3, second, 0)
    head_pieces(12, 4)
    lax.fori_loop(2, 3, third, 0)

    z_rows = pl.ds(pl.multiple_of(z * 8, 8), 8)
    for k in range(3):
        for r in range(1, NZ):
            send_z(k, r).wait_recv()
        total = red[k, :, z_rows, :]
        for r in range(1, NZ) if k < 2 else (2, 4, 6):
            total = total + z_buf[k, r - 1]
        if k < 2:
            fin_own[4 + 2 * k] = total[0]
            fin_own[5 + 2 * k] = total[1]
        else:
            fin_own[parity * 2] = total[0]
            fin_own[parity * 2 + 1] = total[1]
            total = z_buf[k, 0] + z_buf[k, 2] + z_buf[k, 4] + z_buf[k, 6]
            fin_own[(1 - parity) * 2] = total[0]
            fin_own[(1 - parity) * 2 + 1] = total[1]
    fin_core = rdma(fin_own, fin_sib, misc_s.at[4], misc_r.at[4], sib)
    fin_core.start()
    fin_core.wait_recv()
    lower = c == 0
    for j in range(8):
        mine = jnp.where(lower, fin_own[j, 0:4], fin_own[j, 4:8])
        theirs = jnp.where(lower, fin_sib[j, 0:4], fin_sib[j, 4:8])
        hg_out[:, j * WIDE : (j + 1) * WIDE] = jnp.where(lower, mine, theirs).astype(BF16)
        hg_out[:, DHALF + j * WIDE : DHALF + (j + 1) * WIDE] = jnp.where(lower, theirs, mine).astype(BF16)

    for copy in sends + base_swaps + [head_swap, lab_swap, teach_swap, fin_swap, fin_core]:
        copy.wait_send()
    prob_swap(0, xh).wait_send()
    prob_swap(1, 1 - xh).wait_send()
    for r in range(1, VOC):
        stat_voc(t_voc, tv_s, tv_r, r).wait_send()
        stat_voc(s_voc, sv_s, sv_r, r).wait_send()
    for r in range(1, TOK):
        stat_tok(t_tok, tt_s, tt_r, r).wait_send()
        stat_tok(s_tok, st_s, st_r, r).wait_send()
    for n in range(2):
        send_pair(n).wait_send()

    def drain(k, carry):
        for r in range(1, 4):
            send_ya(k, r).wait_send()
            send_yb(k, r).wait_send()
        send_xa(k).wait_send()
        send_xb(k).wait_send()
        for r in range(1, NZ):
            send_z(k, r).wait_send()
        return carry

    lax.fori_loop(0, 3, drain, 0)

    def drain_head(k, carry):
        ho_copy(k).wait()
        return carry

    lax.fori_loop(0, 16, drain_head, 0)


def body(hidden, head, teacher, labels):
    dma = pltpu.SemaphoreType.DMA
    i32 = jnp.int32
    vmem = pltpu.VMEM
    scratch = [
        vmem((ROWS, 16 * WIDE), BF16), vmem((256, COLS), BF16), vmem((2, 128), i32),
        vmem((16, TOKENS, WIDE), BF16),
        vmem((16 * WIDE, COLS), BF16), vmem((DHALF, COLS), BF16),
        vmem((256, COLS), BF16), vmem((2, 128), i32),
        vmem((2, TOKENS, COLS), F32), vmem((2, TOKENS, COLS), F32),
        vmem((TOKENS, 2 * COLS), BF16),
        vmem((VOC, 8, 128), F32), vmem((TOK, 8, 128), F32), vmem((2, 8, 128), F32),
        vmem((VOC, 8, 128), F32), vmem((TOK, 8, 128), F32),
        vmem((8, 2, NY, ROWS, WIDE), BF16), vmem((8, 2, NY, ROWS, WIDE), F32),
        vmem((2, 2, NY, ROWS, WIDE), BF16),
        vmem((3, 3, 2, ROWS, WIDE), BF16),
        vmem((3, ROWS, WIDE), F32), vmem((3, ROWS, WIDE), BF16), vmem((3, ROWS, WIDE), BF16),
        vmem((3, NY, ROWS, WIDE), BF16), vmem((3, NY, ROWS, WIDE), BF16),
        vmem((3, ROWS, WIDE), F32), vmem((3, 3, ROWS, WIDE), BF16),
        vmem((3, 2, ROWS, WIDE), F32), vmem((3, NZ - 1, 2, 8, WIDE), F32),
        vmem((8, 8, WIDE), F32), vmem((8, 8, WIDE), F32),
        vmem((16, WIDE, COLS), BF16),
        dma((7,)), dma((16,)), dma((48,)), dma((48,)), dma((5,)), dma((5,)),
        dma((VOC,)), dma((VOC,)), dma((TOK,)), dma((TOK,)),
        dma((VOC,)), dma((VOC,)), dma((TOK,)), dma((TOK,)),
        dma((4,)), dma((4,)), dma((2,)), dma((2,)),
        dma((3, 4)), dma((3, 4)), dma((3,)), dma((3,)),
        dma((3,)), dma((3,)), dma((3, 4)), dma((3, 4)),
        dma((3, NZ)), dma((3, NZ)),
    ]
    hbm = pl.BlockSpec(memory_space=pltpu.HBM)
    hidden_out, head_out = pl.pallas_call(
        kernel,
        out_shape=(
            jax.ShapeDtypeStruct((4, 16 * WIDE), BF16),
            jax.ShapeDtypeStruct((16 * WIDE, COLS), BF16),
        ),
        in_specs=[hbm] * 4,
        out_specs=(pl.BlockSpec(memory_space=pltpu.VMEM), pl.BlockSpec(memory_space=pl.ANY)),
        scratch_shapes=scratch,
        compiler_params=pltpu.CompilerParams(
            collective_id=0, has_side_effects=True, vmem_limit_bytes=44 << 20
        ),
    )(hidden[0], teacher, labels.reshape(2, 128), head[0])
    return hidden_out[None], head_out[None]


def solution(mesh):
    placed = (
        P("grp", "tok", None),
        P("grp", None, ("tok", "voc")),
        P("grp", ("tok", "voc")),
        P("grp"),
    )
    return jax.shard_map(
        body,
        mesh=mesh,
        in_specs=placed,
        out_specs=(P("grp", ("tok", "voc"), None), P("grp", None, ("tok", "voc"))),
        check_vma=False,
    )
```

```python
import functools

import jax
import jax.numpy as jnp
from jax import lax
from jax.experimental import pallas as pl
from jax.experimental.pallas import tpu as pltpu
from jax.sharding import PartitionSpec as P

GRAD_SCALE = 32.0
KL_WEIGHT = 0.5
MESH = pl.DeviceIdType.MESH
F32 = jnp.float32
BF16 = jnp.bfloat16

NY = 4
NZ = 8
TOK = 2 * NY
VOC = 2 * NZ
ROWS = 64
HALF = NY * ROWS
TOKENS = 2 * HALF
COLS = 640
WIDE = 256
DHALF = 8 * WIDE


def spread(row):
    return jnp.broadcast_to(row, (128, 128)).T


def as_row(col):
    return jnp.broadcast_to(col, (128, 128)).T[0:1, :]


def merge(parts):
    tops = parts[:, 0:4, :]
    top = jnp.max(tops, axis=0)
    total = jnp.sum(parts[:, 4:8, :] * jnp.exp(tops - top[None]), axis=0)
    return jnp.concatenate([top, total], axis=0)


def kernel(
    hid_hbm, teach_hbm, lab_hbm, head_hbm, hg_out, ho_out,
    hid_in, teach_own, lab_own, hid, head_v, head_sib, teach_sib, lab_sib, prob, base, grad,
    t_voc, t_tok, t_fin, s_voc, s_tok,
    part, own, pair_buf, ya_buf, qa_own, qa_send, xa_buf, xb_buf, qb, qb_own, yb_buf, red, z_buf,
    fin_own, fin_sib, ho_buf,
    in_sem, ho_sem, h_s, h_r, misc_s, misc_r, tv_s, tv_r, tt_s, tt_r, sv_s, sv_r, st_s, st_r, pr_s, pr_r,
    pair_s, pair_r, ya_s, ya_r, xa_s, xa_r, xb_s, xb_r, yb_s, yb_r, z_s, z_r,
):
    g = lax.axis_index("grp")
    t = lax.axis_index("tok")
    v = lax.axis_index("voc")
    xh, y = t // NY, t % NY
    z, c = v // 2, v % 2
    parity = z % 2
    sib = (g, t, z * 2 + (1 - c))
    xpart = (g, (1 - xh) * NY + y, v)
    gpart = (1 - g, t, v)

    def ydev(r):
        return (g, xh * NY + lax.rem(y + r, NY), v)

    def zdev(r):
        return (g, t, lax.rem(z + r, NZ) * 2 + c)

    def vdev(r):
        return (g, t, lax.rem(v + r, VOC))

    def tdev(r):
        return (g, lax.rem(t + r, TOK), v)

    def yfrom(r):
        return lax.rem(y + NY - r, NY)

    def rdma(src, dst, ss, rs, device):
        return pltpu.make_async_remote_copy(
            src_ref=src, dst_ref=dst, send_sem=ss, recv_sem=rs, device_id=device, device_id_type=MESH
        )

    def rows_of(col, yy):
        return pl.ds(pl.multiple_of((col * NY + yy) * ROWS, ROWS), ROWS)

    barrier = pltpu.get_barrier_semaphore()
    for r in range(1, VOC):
        pl.semaphore_signal(barrier, inc=1, device_id=vdev(r), device_id_type=MESH)
    for r in range(1, TOK):
        pl.semaphore_signal(barrier, inc=1, device_id=tdev(r), device_id_type=MESH)
    pl.semaphore_signal(barrier, inc=1, device_id=gpart, device_id_type=MESH)

    loads = [
        pltpu.make_async_copy(hid_hbm, hid_in, in_sem.at[0]),
        pltpu.make_async_copy(teach_hbm, teach_own, in_sem.at[1]),
        pltpu.make_async_copy(lab_hbm, lab_own, in_sem.at[2]),
    ]
    for i in range(4):
        rows = pl.ds(i * 1024, 1024)
        loads.append(pltpu.make_async_copy(head_hbm.at[rows, :], head_v.at[rows, :], in_sem.at[3 + i]))
    for load in loads:
        load.start()

    own_rows = rows_of(xh, y)
    loads[0].wait()
    for k in range(16):
        hid[k, own_rows, :] = hid_in[:, k * WIDE : (k + 1) * WIDE]
    loads[1].wait()
    loads[2].wait()

    zero_row = jnp.zeros((1, 128), F32)
    tops, sums = [], []
    for b in range(2):
        vals = teach_own[b * 128 : (b + 1) * 128, :].astype(F32)
        top = jnp.max(vals, axis=1, keepdims=True)
        tops.append(as_row(top))
        sums.append(as_row(jnp.sum(jnp.exp(vals - top), axis=1, keepdims=True)))
    t_voc[0] = jnp.concatenate(tops + [zero_row, zero_row] + sums + [zero_row, zero_row], axis=0)

    pl.semaphore_wait(barrier, VOC + TOK - 1)

    sends = []

    def go(here, device):
        i = len(sends)
        copy = rdma(here, here, h_s.at[i], h_r.at[i], device)
        copy.start()
        sends.append(copy)
        return copy

    first = c * 8 + parity * 4
    other = c * 8 + (1 - parity) * 4

    def chunks(start, n):
        return pl.ds(pl.multiple_of(start, 2), n)

    x_in = go(hid.at[chunks(first, 4), own_rows, :], xpart)
    y_in = {r: go(hid.at[chunks(first, 4), own_rows, :], ydev(r)) for r in (1, 3, 2)}

    def stat_voc(buf, ss, rs, r):
        return rdma(buf.at[0], buf.at[r], ss.at[r], rs.at[r], vdev(r))

    def stat_tok(buf, ss, rs, r):
        return rdma(buf.at[0], buf.at[r], ss.at[r], rs.at[r], tdev(r))

    for r in range(1, VOC):
        stat_voc(t_voc, tv_s, tv_r, r).start()
    sib_rows = pl.ds(pl.multiple_of((1 - c) * DHALF, DHALF), DHALF)
    head_swap = rdma(head_hbm.at[sib_rows, :], head_sib, misc_s.at[0], misc_r.at[0], sib)
    head_swap.start()
    lab_swap = rdma(lab_own, lab_sib, misc_s.at[1], misc_r.at[1], gpart)
    lab_swap.start()
    teach_swap = rdma(teach_own, teach_sib, misc_s.at[2], misc_r.at[2], gpart)

    near, far, z_in = [], [], []

    def share(start, n, rows, arrivals):
        arrivals.append(go(hid.at[chunks(start, n), rows, :], sib))

    def along_z(rows, arrivals, up, down):
        if up:
            copy = go(hid.at[chunks(first, 2), rows, :], zdev(1))
            z_in.append((copy, other, rows, arrivals))
        if down:
            copy = go(hid.at[chunks(first + 2, 2), rows, :], zdev(NZ - 1))
            z_in.append((copy, other + 2, rows, arrivals))

    x_in.wait_recv()
    mirror = rows_of(1 - xh, y)
    a_in = {r: go(hid.at[chunks(first, 2), mirror, :], ydev(r)) for r in (1, 3, 2)}
    along_z(mirror, far, True, True)
    share(first, 4, mirror, far)
    b_in = {}
    for r in (1, 3, 2):
        y_in[r].wait_recv()
        rows = rows_of(xh, yfrom(r))
        b_in[r] = go(hid.at[chunks(first + 2, 2), rows, :], xpart)
        along_z(rows, near, True, True)
        share(first, 4, rows, near)
    teach_swap.start()
    for r in range(1, VOC):
        stat_voc(t_voc, tv_s, tv_r, r).wait_recv()
    t_tok[0] = merge(t_voc[...])
    for r in range(1, TOK):
        stat_tok(t_tok, tt_s, tt_r, r).start()
    for r in (1, 3, 2):
        rows = rows_of(1 - xh, yfrom(r))
        a_in[r].wait_recv()
        along_z(rows, far, True, False)
        share(first, 2, rows, far)
        b_in[r].wait_recv()
        along_z(rows, far, False, True)
        share(first + 2, 2, rows, far)
    for r in range(1, TOK):
        stat_tok(t_tok, tt_s, tt_r, r).wait_recv()
    t_fin[0] = merge(t_tok[...])
    fin_swap = rdma(t_fin.at[0], t_fin.at[1], misc_s.at[3], misc_r.at[3], gpart)
    fin_swap.start()
    for copy, start, rows, arrivals in z_in:
        copy.wait_recv()
        share(start, 2, rows, arrivals)
    for load in loads[3:]:
        load.wait()

    def prob_swap(i, col):
        here = prob.at[c, pl.ds(pl.multiple_of(col * HALF, HALF), HALF), :]
        return rdma(here, here, pr_s.at[i], pr_r.at[i], sib)

    def logits_step(i, carry):
        @pl.when(i == 0)
        def _():
            for copy in near:
                copy.wait_recv()

        @pl.when(i == 1)
        def _():
            for copy in far:
                copy.wait_recv()

        col = jnp.where(i == 0, xh, 1 - xh)
        rows = pl.ds(pl.multiple_of(col * HALF, HALF), HALF)
        lhs = jnp.concatenate([hid[k, rows, :] for k in range(16)], axis=1)
        logits = jnp.dot(lhs, head_v[...], preferred_element_type=F32)
        top = jnp.max(logits, axis=1, keepdims=True)
        expo = jnp.exp(logits - top)
        prob[c, rows, :] = expo
        prob_swap(i, col).start()
        total = jnp.sum(expo, axis=1, keepdims=True)
        for b in range(2):
            at = slice(b * 128, (b + 1) * 128)
            s_voc[0, pl.ds(col * 2 + b, 1), :] = as_row(top[at])
            s_voc[0, pl.ds(4 + col * 2 + b, 1), :] = as_row(total[at])
        return carry

    lax.fori_loop(0, 2, logits_step, 0)

    for r in range(1, VOC):
        stat_voc(s_voc, sv_s, sv_r, r).start()

    lab_swap.wait_recv()
    teach_swap.wait_recv()
    fin_swap.wait_recv()
    column_base = (t * VOC + v) * COLS
    base_swaps = []
    for which in range(2):
        values = teach_own if which == 0 else teach_sib
        labels = lab_own if which == 0 else lab_sib
        row0 = (g if which == 0 else 1 - g) * 256
        for b in range(2):
            rows = pl.ds(pl.multiple_of(row0 + b * 128, 128), 128)
            top = spread(t_fin[which, b : b + 1, :])
            scale = GRAD_SCALE * KL_WEIGHT / spread(t_fin[which, 4 + b : 5 + b, :])
            label = spread(labels[b : b + 1, :])
            for n in range(COLS // 128):
                at = slice(n * 128, (n + 1) * 128)
                soft = jnp.exp(values[b * 128 : (b + 1) * 128, at].astype(F32) - top) * scale
                ids = column_base + n * 128 + lax.broadcasted_iota(jnp.int32, (128, 128), 1)
                base[c, rows, at] = soft + jnp.where(ids == label, GRAD_SCALE * (1.0 - KL_WEIGHT), 0.0)
        here = base.at[c, pl.ds(pl.multiple_of(row0, 256), 256), :]
        base_swaps.append(rdma(here, here, pr_s.at[2 + which], pr_r.at[2 + which], sib))
        base_swaps[-1].start()

    for r in range(1, VOC):
        stat_voc(s_voc, sv_s, sv_r, r).wait_recv()
    s_tok[0] = merge(s_voc[...])
    for r in range(1, TOK):
        stat_tok(s_tok, st_s, st_r, r).start()
    head_swap.wait_recv()
    prob_swap(0, xh).wait_recv()
    prob_swap(1, 1 - xh).wait_recv()
    for copy in base_swaps:
        copy.wait_recv()
    for r in range(1, TOK):
        stat_tok(s_tok, st_s, st_r, r).wait_recv()
    final = merge(s_tok[...])
    sib_slot = jnp.where(c == 1, 1, VOC - 1)
    for which in range(2):
        tops = s_voc[0, 0:4, :] if which == 0 else s_voc[sib_slot, 0:4, :]
        core = c if which == 0 else 1 - c
        factor = GRAD_SCALE * jnp.exp(tops - final[0:4, :]) / final[4:8, :]
        for b in range(4):
            rows = slice(b * 128, (b + 1) * 128)
            mat = spread(factor[b : b + 1, :])
            for n in range(COLS // 128):
                at = slice(n * 128, (n + 1) * 128)
                out = prob[core, rows, at] * mat - base[core, rows, at]
                grad[rows, which * COLS + n * 128 : which * COLS + (n + 1) * 128] = out.astype(BF16)

    def chunk_of(i):
        return jnp.where(i < 2, (1 - parity) * 2 + i, jnp.where(i < 6, i + 2, parity * 2 + i - 6))

    def send_pair(i):
        return rdma(part.at[i], pair_buf.at[i], pair_s.at[i], pair_r.at[i], zdev(1 if i == 0 else NZ - 1))

    def send_ya(k, r):
        return rdma(
            part.at[2 + 2 * k, :, lax.rem(y + r, NY)], ya_buf.at[k, r - 1], ya_s.at[k, r], ya_r.at[k, r], ydev(r)
        )

    def send_xb(k):
        return rdma(part.at[3 + 2 * k, 1 - xh], xb_buf.at[k], xb_s.at[k], xb_r.at[k], xpart)

    def send_xa(k):
        return rdma(qa_send.at[k], xa_buf.at[k], xa_s.at[k], xa_r.at[k], xpart)

    def send_yb(k, r):
        return rdma(qb.at[k, lax.rem(y + r, NY)], yb_buf.at[k, r - 1], yb_s.at[k, r], yb_r.at[k, r], ydev(r))

    def send_z(k, r):
        rows = pl.ds(pl.multiple_of(lax.rem(z + r, NZ) * 8, 8), 8)
        return rdma(red.at[k, :, rows, :], z_buf.at[k, r - 1], z_s.at[k, r], z_r.at[k, r], zdev(r))

    def ho_copy(k):
        return pltpu.make_async_copy(
            ho_buf.at[k], ho_out.at[pl.ds(pl.multiple_of(k * WIDE, WIDE), WIDE), :], ho_sem.at[k]
        )

    def head_pieces(start, n):
        def piece(k, carry):
            out = lax.dot_general(
                hid[k], grad[:, 0:COLS], (((0,), (0,)), ((), ())), preferred_element_type=F32
            )
            ho_buf[k] = out.astype(BF16)
            ho_copy(k).start()
            return carry

        lax.fori_loop(start, start + n, piece, 0)

    def product(i, carry):
        j = chunk_of(i)
        left = head_v[pl.ds(pl.multiple_of(c * DHALF + j * WIDE, WIDE), WIDE), :]
        right = head_sib[pl.ds(pl.multiple_of(j * WIDE, WIDE), WIDE), :]
        rhs = jnp.concatenate([left, right], axis=1)
        out = lax.dot_general(grad[...], rhs, (((1,), (1,)), ((), ())), preferred_element_type=F32)
        out = out.reshape(2, NY, ROWS, WIDE)
        own[i] = out
        part[i] = out.astype(BF16)

        for n in range(2):

            @pl.when(i == n)
            def _():
                send_pair(n).start()

            @pl.when(i == 2 + 2 * n)
            def _():
                for r in (1, 3, 2):
                    send_ya(n, r).start()

            @pl.when(i == 3 + 2 * n)
            def _():
                send_xb(n).start()

        return carry

    lax.fori_loop(0, 8, product, 0)

    def second(k, carry):
        for r in (1, 3, 2):
            send_ya(k, r).wait_recv()

        def column(col):
            total = own[2 + 2 * k, col, y]
            for r in range(3):
                total = total + ya_buf[k, r, col].astype(F32)
            return total

        qa_send[k] = column(1 - xh).astype(BF16)
        send_xa(k).start()
        qa_own[k] = column(xh)
        send_xb(k).wait_recv()
        qb[k] = (own[3 + 2 * k, xh] + xb_buf[k].astype(F32)).astype(BF16)
        for r in (1, 3, 2):
            send_yb(k, r).start()
        qb_own[k] = own[3 + 2 * k, xh, y] + xb_buf[k, y].astype(F32)
        return carry

    def third(k, carry):
        send_xa(k).wait_recv()
        red[k, 0] = qa_own[k] + xa_buf[k].astype(F32)
        for r in (1, 3, 2):
            send_yb(k, r).wait_recv()
        total = qb_own[k]
        for r in range(3):
            total = total + yb_buf[k, r].astype(F32)
        red[k, 1] = total
        for r in (4, 3, 5, 2, 6, 1, 7):
            send_z(k, r).start()
        return carry

    head_pieces(0, 3)
    lax.fori_loop(0, 1, second, 0)
    for copy in sends + base_swaps + [head_swap, lab_swap, teach_swap, fin_swap]:
        copy.wait_send()
    for n in range(2):
        send_pair(n).wait_recv()
        total = own[6 + n] + pair_buf[n].astype(F32)
        own[6 + n] = total
        part[6 + n] = total.astype(BF16)
        if n == 0:
            for r in (1, 3, 2):
                send_ya(2, r).start()
        else:
            send_xb(2).start()
    lax.fori_loop(1, 2, second, 0)
    head_pieces(3, 3)
    lax.fori_loop(0, 1, third, 0)
    head_pieces(6, 4)
    lax.fori_loop(1, 2, third, 0)
    lax.fori_loop(2, 3, second, 0)
    head_pieces(10, 4)
    lax.fori_loop(2, 3, third, 0)
    head_pieces(14, 2)
    prob_swap(0, xh).wait_send()
    prob_swap(1, 1 - xh).wait_send()
    for r in range(1, VOC):
        stat_voc(t_voc, tv_s, tv_r, r).wait_send()
        stat_voc(s_voc, sv_s, sv_r, r).wait_send()
    for r in range(1, TOK):
        stat_tok(t_tok, tt_s, tt_r, r).wait_send()
        stat_tok(s_tok, st_s, st_r, r).wait_send()

    def drain(k, carry):
        for r in range(1, 4):
            send_ya(k, r).wait_send()
            send_yb(k, r).wait_send()
        send_xa(k).wait_send()
        send_xb(k).wait_send()
        return carry

    lax.fori_loop(0, 3, drain, 0)
    for n in range(2):
        send_pair(n).wait_send()

    z_rows = pl.ds(pl.multiple_of(z * 8, 8), 8)
    for k in range(3):
        for r in range(1, NZ):
            send_z(k, r).wait_recv()
        total = red[k, :, z_rows, :]
        for r in range(1, NZ) if k < 2 else (2, 4, 6):
            total = total + z_buf[k, r - 1]
        if k < 2:
            fin_own[4 + 2 * k] = total[0]
            fin_own[5 + 2 * k] = total[1]
        else:
            fin_own[parity * 2] = total[0]
            fin_own[parity * 2 + 1] = total[1]
            total = z_buf[k, 0] + z_buf[k, 2] + z_buf[k, 4] + z_buf[k, 6]
            fin_own[(1 - parity) * 2] = total[0]
            fin_own[(1 - parity) * 2 + 1] = total[1]
    fin_core = rdma(fin_own, fin_sib, misc_s.at[4], misc_r.at[4], sib)
    fin_core.start()
    fin_core.wait_recv()
    lower = c == 0
    for j in range(8):
        mine = jnp.where(lower, fin_own[j, 0:4], fin_own[j, 4:8])
        theirs = jnp.where(lower, fin_sib[j, 0:4], fin_sib[j, 4:8])
        hg_out[:, j * WIDE : (j + 1) * WIDE] = jnp.where(lower, mine, theirs).astype(BF16)
        hg_out[:, DHALF + j * WIDE : DHALF + (j + 1) * WIDE] = jnp.where(lower, theirs, mine).astype(BF16)

    fin_core.wait_send()

    def drain_z(k, carry):
        for r in range(1, NZ):
            send_z(k, r).wait_send()
        return carry

    lax.fori_loop(0, 3, drain_z, 0)

    def drain_head(k, carry):
        ho_copy(k).wait()
        return carry

    lax.fori_loop(0, 16, drain_head, 0)


def body(hidden, head, teacher, labels):
    dma = pltpu.SemaphoreType.DMA
    i32 = jnp.int32
    vmem = pltpu.VMEM
    scratch = [
        vmem((ROWS, 16 * WIDE), BF16), vmem((256, COLS), BF16), vmem((2, 128), i32),
        vmem((16, TOKENS, WIDE), BF16),
        vmem((16 * WIDE, COLS), BF16), vmem((DHALF, COLS), BF16),
        vmem((256, COLS), BF16), vmem((2, 128), i32),
        vmem((2, TOKENS, COLS), F32), vmem((2, TOKENS, COLS), F32),
        vmem((TOKENS, 2 * COLS), BF16),
        vmem((VOC, 8, 128), F32), vmem((TOK, 8, 128), F32), vmem((2, 8, 128), F32),
        vmem((VOC, 8, 128), F32), vmem((TOK, 8, 128), F32),
        vmem((8, 2, NY, ROWS, WIDE), BF16), vmem((8, 2, NY, ROWS, WIDE), F32),
        vmem((2, 2, NY, ROWS, WIDE), BF16),
        vmem((3, 3, 2, ROWS, WIDE), BF16),
        vmem((3, ROWS, WIDE), F32), vmem((3, ROWS, WIDE), BF16), vmem((3, ROWS, WIDE), BF16),
        vmem((3, NY, ROWS, WIDE), BF16), vmem((3, NY, ROWS, WIDE), BF16),
        vmem((3, ROWS, WIDE), F32), vmem((3, 3, ROWS, WIDE), BF16),
        vmem((3, 2, ROWS, WIDE), F32), vmem((3, NZ - 1, 2, 8, WIDE), F32),
        vmem((8, 8, WIDE), F32), vmem((8, 8, WIDE), F32),
        vmem((16, WIDE, COLS), BF16),
        dma((7,)), dma((16,)), dma((48,)), dma((48,)), dma((5,)), dma((5,)),
        dma((VOC,)), dma((VOC,)), dma((TOK,)), dma((TOK,)),
        dma((VOC,)), dma((VOC,)), dma((TOK,)), dma((TOK,)),
        dma((4,)), dma((4,)), dma((2,)), dma((2,)),
        dma((3, 4)), dma((3, 4)), dma((3,)), dma((3,)),
        dma((3,)), dma((3,)), dma((3, 4)), dma((3, 4)),
        dma((3, NZ)), dma((3, NZ)),
    ]
    hbm = pl.BlockSpec(memory_space=pltpu.HBM)
    hidden_out, head_out = pl.pallas_call(
        kernel,
        out_shape=(
            jax.ShapeDtypeStruct((4, 16 * WIDE), BF16),
            jax.ShapeDtypeStruct((16 * WIDE, COLS), BF16),
        ),
        in_specs=[hbm] * 4,
        out_specs=(pl.BlockSpec(memory_space=pltpu.VMEM), pl.BlockSpec(memory_space=pl.ANY)),
        scratch_shapes=scratch,
        compiler_params=pltpu.CompilerParams(
            collective_id=0, has_side_effects=True, vmem_limit_bytes=44 << 20
        ),
    )(hidden[0], teacher, labels.reshape(2, 128), head[0])
    return hidden_out[None], head_out[None]


def solution(mesh):
    placed = (
        P("grp", "tok", None),
        P("grp", None, ("tok", "voc")),
        P("grp", ("tok", "voc")),
        P("grp"),
    )
    return jax.shard_map(
        body,
        mesh=mesh,
        in_specs=placed,
        out_specs=(P("grp", ("tok", "voc"), None), P("grp", None, ("tok", "voc"))),
        check_vma=False,
    )
```

```python
import functools

import jax
import jax.numpy as jnp
from jax import lax
from jax.experimental import pallas as pl
from jax.experimental.pallas import tpu as pltpu
from jax.sharding import PartitionSpec as P

GRAD_SCALE = 32.0
KL_WEIGHT = 0.5
MESH = pl.DeviceIdType.MESH
F32 = jnp.float32
BF16 = jnp.bfloat16

NY = 4
NZ = 8
TOK = 2 * NY
VOC = 2 * NZ
ROWS = 64
HALF = NY * ROWS
TOKENS = 2 * HALF
COLS = 640
WIDE = 256
DHALF = 8 * WIDE


def spread(row):
    return jnp.broadcast_to(row, (128, 128)).T


def as_row(col):
    return jnp.broadcast_to(col, (128, 128)).T[0:1, :]


def merge(parts):
    tops = parts[:, 0:4, :]
    top = jnp.max(tops, axis=0)
    total = jnp.sum(parts[:, 4:8, :] * jnp.exp(tops - top[None]), axis=0)
    return jnp.concatenate([top, total], axis=0)


def kernel(
    hid_hbm, teach_hbm, lab_hbm, head_hbm, hg_out, ho_out,
    hid_in, teach_own, lab_own, hid, head_v, head_sib, teach_sib, lab_sib, prob, base, grad,
    t_voc, t_tok, t_fin, s_voc, s_tok,
    part, own, pair_buf, ya_buf, qa_own, qa_send, xa_buf, xb_buf, qb, qb_own, yb_buf, red, z_buf,
    fin_own, fin_sib, ho_buf,
    in_sem, ho_sem, h_s, h_r, misc_s, misc_r, tv_s, tv_r, tt_s, tt_r, sv_s, sv_r, st_s, st_r, pr_s, pr_r,
    pair_s, pair_r, ya_s, ya_r, xa_s, xa_r, xb_s, xb_r, yb_s, yb_r, z_s, z_r,
):
    g = lax.axis_index("grp")
    t = lax.axis_index("tok")
    v = lax.axis_index("voc")
    xh, y = t // NY, t % NY
    z, c = v // 2, v % 2
    parity = z % 2
    sib = (g, t, z * 2 + (1 - c))
    xpart = (g, (1 - xh) * NY + y, v)
    gpart = (1 - g, t, v)

    def ydev(r):
        return (g, xh * NY + lax.rem(y + r, NY), v)

    def zdev(r):
        return (g, t, lax.rem(z + r, NZ) * 2 + c)

    def vdev(r):
        return (g, t, lax.rem(v + r, VOC))

    def tdev(r):
        return (g, lax.rem(t + r, TOK), v)

    def yfrom(r):
        return lax.rem(y + NY - r, NY)

    def rdma(src, dst, ss, rs, device):
        return pltpu.make_async_remote_copy(
            src_ref=src, dst_ref=dst, send_sem=ss, recv_sem=rs, device_id=device, device_id_type=MESH
        )

    def rows_of(col, yy):
        return pl.ds(pl.multiple_of((col * NY + yy) * ROWS, ROWS), ROWS)

    barrier = pltpu.get_barrier_semaphore()
    for r in range(1, VOC):
        pl.semaphore_signal(barrier, inc=1, device_id=vdev(r), device_id_type=MESH)
    for r in range(1, TOK):
        pl.semaphore_signal(barrier, inc=1, device_id=tdev(r), device_id_type=MESH)
    pl.semaphore_signal(barrier, inc=1, device_id=gpart, device_id_type=MESH)

    loads = [
        pltpu.make_async_copy(hid_hbm, hid_in, in_sem.at[0]),
        pltpu.make_async_copy(teach_hbm, teach_own, in_sem.at[1]),
        pltpu.make_async_copy(lab_hbm, lab_own, in_sem.at[2]),
    ]
    for i in range(4):
        rows = pl.ds(i * 1024, 1024)
        loads.append(pltpu.make_async_copy(head_hbm.at[rows, :], head_v.at[rows, :], in_sem.at[3 + i]))
    for load in loads:
        load.start()

    own_rows = rows_of(xh, y)
    loads[0].wait()
    for k in range(16):
        hid[k, own_rows, :] = hid_in[:, k * WIDE : (k + 1) * WIDE]
    loads[1].wait()
    loads[2].wait()

    zero_row = jnp.zeros((1, 128), F32)
    tops, sums = [], []
    for b in range(2):
        vals = teach_own[b * 128 : (b + 1) * 128, :].astype(F32)
        top = jnp.max(vals, axis=1, keepdims=True)
        tops.append(as_row(top))
        sums.append(as_row(jnp.sum(jnp.exp(vals - top), axis=1, keepdims=True)))
    t_voc[0] = jnp.concatenate(tops + [zero_row, zero_row] + sums + [zero_row, zero_row], axis=0)

    pl.semaphore_wait(barrier, VOC + TOK - 1)

    sends = []

    def go(here, device):
        i = len(sends)
        copy = rdma(here, here, h_s.at[i], h_r.at[i], device)
        copy.start()
        sends.append(copy)
        return copy

    first = c * 8 + parity * 4
    other = c * 8 + (1 - parity) * 4

    def chunks(start, n):
        return pl.ds(pl.multiple_of(start, 2), n)

    x_in = go(hid.at[chunks(first, 4), own_rows, :], xpart)
    y_in = {r: go(hid.at[chunks(first, 4), own_rows, :], ydev(r)) for r in (1, 3, 2)}

    def stat_voc(buf, ss, rs, r):
        return rdma(buf.at[0], buf.at[r], ss.at[r], rs.at[r], vdev(r))

    def stat_tok(buf, ss, rs, r):
        return rdma(buf.at[0], buf.at[r], ss.at[r], rs.at[r], tdev(r))

    for r in range(1, VOC):
        stat_voc(t_voc, tv_s, tv_r, r).start()
    sib_rows = pl.ds(pl.multiple_of((1 - c) * DHALF, DHALF), DHALF)
    head_swap = rdma(head_hbm.at[sib_rows, :], head_sib, misc_s.at[0], misc_r.at[0], sib)
    head_swap.start()
    lab_swap = rdma(lab_own, lab_sib, misc_s.at[1], misc_r.at[1], gpart)
    lab_swap.start()
    teach_swap = rdma(teach_own, teach_sib, misc_s.at[2], misc_r.at[2], gpart)

    near, far, z_in = [], [], []

    def share(start, n, rows, arrivals):
        arrivals.append(go(hid.at[chunks(start, n), rows, :], sib))

    def along_z(rows, arrivals, up, down):
        if up:
            copy = go(hid.at[chunks(first, 2), rows, :], zdev(1))
            z_in.append((copy, other, rows, arrivals))
        if down:
            copy = go(hid.at[chunks(first + 2, 2), rows, :], zdev(NZ - 1))
            z_in.append((copy, other + 2, rows, arrivals))

    x_in.wait_recv()
    mirror = rows_of(1 - xh, y)
    a_in = {r: go(hid.at[chunks(first, 2), mirror, :], ydev(r)) for r in (1, 3, 2)}
    along_z(mirror, far, True, True)
    share(first, 4, mirror, far)
    b_in = {}
    for r in (1, 3, 2):
        y_in[r].wait_recv()
        rows = rows_of(xh, yfrom(r))
        b_in[r] = go(hid.at[chunks(first + 2, 2), rows, :], xpart)
        along_z(rows, near, True, True)
        share(first, 4, rows, near)
    teach_swap.start()
    for r in range(1, VOC):
        stat_voc(t_voc, tv_s, tv_r, r).wait_recv()
    t_tok[0] = merge(t_voc[...])
    for r in range(1, TOK):
        stat_tok(t_tok, tt_s, tt_r, r).start()
    for r in (1, 3, 2):
        rows = rows_of(1 - xh, yfrom(r))
        a_in[r].wait_recv()
        along_z(rows, far, True, False)
        share(first, 2, rows, far)
        b_in[r].wait_recv()
        along_z(rows, far, False, True)
        share(first + 2, 2, rows, far)
    for r in range(1, TOK):
        stat_tok(t_tok, tt_s, tt_r, r).wait_recv()
    t_fin[0] = merge(t_tok[...])
    fin_swap = rdma(t_fin.at[0], t_fin.at[1], misc_s.at[3], misc_r.at[3], gpart)
    fin_swap.start()
    for copy, start, rows, arrivals in z_in:
        copy.wait_recv()
        share(start, 2, rows, arrivals)
    for load in loads[3:]:
        load.wait()

    def prob_swap(i, col):
        here = prob.at[c, pl.ds(pl.multiple_of(col * HALF, HALF), HALF), :]
        return rdma(here, here, pr_s.at[i], pr_r.at[i], sib)

    def logits_step(i, carry):
        @pl.when(i == 0)
        def _():
            for copy in near:
                copy.wait_recv()

        @pl.when(i == 1)
        def _():
            for copy in far:
                copy.wait_recv()

        col = jnp.where(i == 0, xh, 1 - xh)
        rows = pl.ds(pl.multiple_of(col * HALF, HALF), HALF)
        lhs = jnp.concatenate([hid[k, rows, :] for k in range(16)], axis=1)
        logits = jnp.dot(lhs, head_v[...], preferred_element_type=F32)
        top = jnp.max(logits, axis=1, keepdims=True)
        expo = jnp.exp(logits - top)
        prob[c, rows, :] = expo
        prob_swap(i, col).start()
        total = jnp.sum(expo, axis=1, keepdims=True)
        for b in range(2):
            at = slice(b * 128, (b + 1) * 128)
            s_voc[0, pl.ds(col * 2 + b, 1), :] = as_row(top[at])
            s_voc[0, pl.ds(4 + col * 2 + b, 1), :] = as_row(total[at])
        return carry

    lax.fori_loop(0, 2, logits_step, 0)

    for r in range(1, VOC):
        stat_voc(s_voc, sv_s, sv_r, r).start()

    lab_swap.wait_recv()
    teach_swap.wait_recv()
    fin_swap.wait_recv()
    column_base = (t * VOC + v) * COLS
    base_swaps = []
    for which in range(2):
        values = teach_own if which == 0 else teach_sib
        labels = lab_own if which == 0 else lab_sib
        row0 = (g if which == 0 else 1 - g) * 256
        for b in range(2):
            rows = pl.ds(pl.multiple_of(row0 + b * 128, 128), 128)
            top = spread(t_fin[which, b : b + 1, :])
            scale = GRAD_SCALE * KL_WEIGHT / spread(t_fin[which, 4 + b : 5 + b, :])
            label = spread(labels[b : b + 1, :])
            for n in range(COLS // 128):
                at = slice(n * 128, (n + 1) * 128)
                soft = jnp.exp(values[b * 128 : (b + 1) * 128, at].astype(F32) - top) * scale
                ids = column_base + n * 128 + lax.broadcasted_iota(jnp.int32, (128, 128), 1)
                base[c, rows, at] = soft + jnp.where(ids == label, GRAD_SCALE * (1.0 - KL_WEIGHT), 0.0)
        here = base.at[c, pl.ds(pl.multiple_of(row0, 256), 256), :]
        base_swaps.append(rdma(here, here, pr_s.at[2 + which], pr_r.at[2 + which], sib))
        base_swaps[-1].start()

    for r in range(1, VOC):
        stat_voc(s_voc, sv_s, sv_r, r).wait_recv()
    s_tok[0] = merge(s_voc[...])
    for r in range(1, TOK):
        stat_tok(s_tok, st_s, st_r, r).start()
    head_swap.wait_recv()
    prob_swap(0, xh).wait_recv()
    prob_swap(1, 1 - xh).wait_recv()
    for copy in base_swaps:
        copy.wait_recv()
    for r in range(1, TOK):
        stat_tok(s_tok, st_s, st_r, r).wait_recv()
    final = merge(s_tok[...])
    sib_slot = jnp.where(c == 1, 1, VOC - 1)
    for which in range(2):
        tops = s_voc[0, 0:4, :] if which == 0 else s_voc[sib_slot, 0:4, :]
        core = c if which == 0 else 1 - c
        factor = GRAD_SCALE * jnp.exp(tops - final[0:4, :]) / final[4:8, :]
        for b in range(4):
            rows = slice(b * 128, (b + 1) * 128)
            mat = spread(factor[b : b + 1, :])
            for n in range(COLS // 128):
                at = slice(n * 128, (n + 1) * 128)
                out = prob[core, rows, at] * mat - base[core, rows, at]
                grad[rows, which * COLS + n * 128 : which * COLS + (n + 1) * 128] = out.astype(BF16)

    def chunk_of(i):
        return jnp.where(i < 2, (1 - parity) * 2 + i, jnp.where(i < 6, i + 2, parity * 2 + i - 6))

    def send_pair_a(r):
        yy = lax.rem(y + r, NY)
        return rdma(part.at[0, :, yy], pair_buf.at[0, :, yy], pair_s.at[0, r], pair_r.at[0, r], zdev(1))

    def send_pair_b(h):
        col = 1 - xh if h == 0 else xh
        return rdma(part.at[1, col], pair_buf.at[1, col], pair_s.at[1, h], pair_r.at[1, h], zdev(NZ - 1))

    def send_ya(k, r):
        return rdma(
            part.at[2 + 2 * k, :, lax.rem(y + r, NY)], ya_buf.at[k, r - 1], ya_s.at[k, r], ya_r.at[k, r], ydev(r)
        )

    def send_xb(k):
        return rdma(part.at[3 + 2 * k, 1 - xh], xb_buf.at[k], xb_s.at[k], xb_r.at[k], xpart)

    def send_xa(k):
        return rdma(qa_send.at[k], xa_buf.at[k], xa_s.at[k], xa_r.at[k], xpart)

    def send_yb(k, r):
        return rdma(qb.at[k, lax.rem(y + r, NY)], yb_buf.at[k, r - 1], yb_s.at[k, r], yb_r.at[k, r], ydev(r))

    def send_z(k, r):
        rows = pl.ds(pl.multiple_of(lax.rem(z + r, NZ) * 8, 8), 8)
        return rdma(red.at[k, :, rows, :], z_buf.at[k, r - 1], z_s.at[k, r], z_r.at[k, r], zdev(r))

    def ho_copy(k):
        return pltpu.make_async_copy(
            ho_buf.at[k], ho_out.at[pl.ds(pl.multiple_of(k * WIDE, WIDE), WIDE), :], ho_sem.at[k]
        )

    def head_pieces(start, n):
        def piece(k, carry):
            out = lax.dot_general(
                hid[k], grad[:, 0:COLS], (((0,), (0,)), ((), ())), preferred_element_type=F32
            )
            ho_buf[k] = out.astype(BF16)
            ho_copy(k).start()
            return carry

        lax.fori_loop(start, start + n, piece, 0)

    def product(i, carry):
        j = chunk_of(i)
        left = head_v[pl.ds(pl.multiple_of(c * DHALF + j * WIDE, WIDE), WIDE), :]
        right = head_sib[pl.ds(pl.multiple_of(j * WIDE, WIDE), WIDE), :]
        rhs = jnp.concatenate([left, right], axis=1)
        out = lax.dot_general(grad[...], rhs, (((1,), (1,)), ((), ())), preferred_element_type=F32)
        out = out.reshape(2, NY, ROWS, WIDE)
        own[i] = out
        part[i] = out.astype(BF16)

        for n in range(2):

            @pl.when(i == n)
            def _():
                if n == 0:
                    for r in (2, 1, 3, 0):
                        send_pair_a(r).start()
                else:
                    for h in range(2):
                        send_pair_b(h).start()

            @pl.when(i == 2 + 2 * n)
            def _():
                for r in (1, 3, 2):
                    send_ya(n, r).start()

            @pl.when(i == 3 + 2 * n)
            def _():
                send_xb(n).start()

        return carry

    lax.fori_loop(0, 8, product, 0)

    def second(k, carry):
        for r in (1, 3, 2):
            send_ya(k, r).wait_recv()

        def column(col):
            total = own[2 + 2 * k, col, y]
            for r in range(3):
                total = total + ya_buf[k, r, col].astype(F32)
            return total

        qa_send[k] = column(1 - xh).astype(BF16)
        send_xa(k).start()
        qa_own[k] = column(xh)
        send_xb(k).wait_recv()
        qb[k] = (own[3 + 2 * k, xh] + xb_buf[k].astype(F32)).astype(BF16)
        for r in (1, 3, 2):
            send_yb(k, r).start()
        qb_own[k] = own[3 + 2 * k, xh, y] + xb_buf[k, y].astype(F32)
        return carry

    def third(k, carry):
        send_xa(k).wait_recv()
        red[k, 0] = qa_own[k] + xa_buf[k].astype(F32)
        for r in (1, 3, 2):
            send_yb(k, r).wait_recv()
        total = qb_own[k]
        for r in range(3):
            total = total + yb_buf[k, r].astype(F32)
        red[k, 1] = total
        for r in (4, 3, 5, 2, 6, 1, 7):
            send_z(k, r).start()
        return carry

    head_pieces(0, 2)
    for r in (2, 1, 3):
        send_pair_a(r).wait_recv()
        yy = lax.rem(y + r, NY)
        for col in range(2):
            part[6, col, yy] = (own[6, col, yy] + pair_buf[0, col, yy].astype(F32)).astype(BF16)
        send_ya(2, r).start()
    send_pair_b(0).wait_recv()
    part[7, 1 - xh] = (own[7, 1 - xh] + pair_buf[1, 1 - xh].astype(F32)).astype(BF16)
    send_xb(2).start()
    lax.fori_loop(0, 1, second, 0)
    send_pair_a(0).wait_recv()
    for col in range(2):
        own[6, col, y] = own[6, col, y] + pair_buf[0, col, y].astype(F32)
    send_pair_b(1).wait_recv()
    own[7, xh] = own[7, xh] + pair_buf[1, xh].astype(F32)
    head_pieces(2, 1)
    for copy in sends + base_swaps + [head_swap, lab_swap, teach_swap, fin_swap]:
        copy.wait_send()
    lax.fori_loop(1, 2, second, 0)
    head_pieces(3, 3)
    lax.fori_loop(0, 1, third, 0)
    head_pieces(6, 4)
    lax.fori_loop(1, 2, third, 0)
    lax.fori_loop(2, 3, second, 0)
    head_pieces(10, 4)
    lax.fori_loop(2, 3, third, 0)
    head_pieces(14, 2)
    prob_swap(0, xh).wait_send()
    prob_swap(1, 1 - xh).wait_send()
    for r in range(1, VOC):
        stat_voc(t_voc, tv_s, tv_r, r).wait_send()
        stat_voc(s_voc, sv_s, sv_r, r).wait_send()
    for r in range(1, TOK):
        stat_tok(t_tok, tt_s, tt_r, r).wait_send()
        stat_tok(s_tok, st_s, st_r, r).wait_send()

    def drain(k, carry):
        for r in range(1, 4):
            send_ya(k, r).wait_send()
            send_yb(k, r).wait_send()
        send_xa(k).wait_send()
        send_xb(k).wait_send()
        return carry

    lax.fori_loop(0, 3, drain, 0)
    for r in range(4):
        send_pair_a(r).wait_send()
    for h in range(2):
        send_pair_b(h).wait_send()

    z_rows = pl.ds(pl.multiple_of(z * 8, 8), 8)
    for k in range(3):
        for r in range(1, NZ):
            send_z(k, r).wait_recv()
        total = red[k, :, z_rows, :]
        for r in range(1, NZ) if k < 2 else (2, 4, 6):
            total = total + z_buf[k, r - 1]
        if k < 2:
            fin_own[4 + 2 * k] = total[0]
            fin_own[5 + 2 * k] = total[1]
        else:
            fin_own[parity * 2] = total[0]
            fin_own[parity * 2 + 1] = total[1]
            total = z_buf[k, 0] + z_buf[k, 2] + z_buf[k, 4] + z_buf[k, 6]
            fin_own[(1 - parity) * 2] = total[0]
            fin_own[(1 - parity) * 2 + 1] = total[1]
    fin_core = rdma(fin_own, fin_sib, misc_s.at[4], misc_r.at[4], sib)
    fin_core.start()
    fin_core.wait_recv()
    lower = c == 0
    for j in range(8):
        mine = jnp.where(lower, fin_own[j, 0:4], fin_own[j, 4:8])
        theirs = jnp.where(lower, fin_sib[j, 0:4], fin_sib[j, 4:8])
        hg_out[:, j * WIDE : (j + 1) * WIDE] = jnp.where(lower, mine, theirs).astype(BF16)
        hg_out[:, DHALF + j * WIDE : DHALF + (j + 1) * WIDE] = jnp.where(lower, theirs, mine).astype(BF16)

    fin_core.wait_send()

    def drain_z(k, carry):
        for r in range(1, NZ):
            send_z(k, r).wait_send()
        return carry

    lax.fori_loop(0, 3, drain_z, 0)

    def drain_head(k, carry):
        ho_copy(k).wait()
        return carry

    lax.fori_loop(0, 16, drain_head, 0)


def body(hidden, head, teacher, labels):
    dma = pltpu.SemaphoreType.DMA
    i32 = jnp.int32
    vmem = pltpu.VMEM
    scratch = [
        vmem((ROWS, 16 * WIDE), BF16), vmem((256, COLS), BF16), vmem((2, 128), i32),
        vmem((16, TOKENS, WIDE), BF16),
        vmem((16 * WIDE, COLS), BF16), vmem((DHALF, COLS), BF16),
        vmem((256, COLS), BF16), vmem((2, 128), i32),
        vmem((2, TOKENS, COLS), F32), vmem((2, TOKENS, COLS), F32),
        vmem((TOKENS, 2 * COLS), BF16),
        vmem((VOC, 8, 128), F32), vmem((TOK, 8, 128), F32), vmem((2, 8, 128), F32),
        vmem((VOC, 8, 128), F32), vmem((TOK, 8, 128), F32),
        vmem((8, 2, NY, ROWS, WIDE), BF16), vmem((8, 2, NY, ROWS, WIDE), F32),
        vmem((2, 2, NY, ROWS, WIDE), BF16),
        vmem((3, 3, 2, ROWS, WIDE), BF16),
        vmem((3, ROWS, WIDE), F32), vmem((3, ROWS, WIDE), BF16), vmem((3, ROWS, WIDE), BF16),
        vmem((3, NY, ROWS, WIDE), BF16), vmem((3, NY, ROWS, WIDE), BF16),
        vmem((3, ROWS, WIDE), F32), vmem((3, 3, ROWS, WIDE), BF16),
        vmem((3, 2, ROWS, WIDE), F32), vmem((3, NZ - 1, 2, 8, WIDE), F32),
        vmem((8, 8, WIDE), F32), vmem((8, 8, WIDE), F32),
        vmem((16, WIDE, COLS), BF16),
        dma((7,)), dma((16,)), dma((48,)), dma((48,)), dma((5,)), dma((5,)),
        dma((VOC,)), dma((VOC,)), dma((TOK,)), dma((TOK,)),
        dma((VOC,)), dma((VOC,)), dma((TOK,)), dma((TOK,)),
        dma((4,)), dma((4,)), dma((2, 4)), dma((2, 4)),
        dma((3, 4)), dma((3, 4)), dma((3,)), dma((3,)),
        dma((3,)), dma((3,)), dma((3, 4)), dma((3, 4)),
        dma((3, NZ)), dma((3, NZ)),
    ]
    hbm = pl.BlockSpec(memory_space=pltpu.HBM)
    hidden_out, head_out = pl.pallas_call(
        kernel,
        out_shape=(
            jax.ShapeDtypeStruct((4, 16 * WIDE), BF16),
            jax.ShapeDtypeStruct((16 * WIDE, COLS), BF16),
        ),
        in_specs=[hbm] * 4,
        out_specs=(pl.BlockSpec(memory_space=pltpu.VMEM), pl.BlockSpec(memory_space=pl.ANY)),
        scratch_shapes=scratch,
        compiler_params=pltpu.CompilerParams(
            collective_id=0, has_side_effects=True, vmem_limit_bytes=44 << 20
        ),
    )(hidden[0], teacher, labels.reshape(2, 128), head[0])
    return hidden_out[None], head_out[None]


def solution(mesh):
    placed = (
        P("grp", "tok", None),
        P("grp", None, ("tok", "voc")),
        P("grp", ("tok", "voc")),
        P("grp"),
    )
    return jax.shard_map(
        body,
        mesh=mesh,
        in_specs=placed,
        out_specs=(P("grp", ("tok", "voc"), None), P("grp", None, ("tok", "voc"))),
        check_vma=False,
    )
```
